32 devices in a mesh: ctx: 16 (over z, y, x), kvh: 2 (over core).
Axes of the slice: x: 2, y: 2, z: 4, core: 2. Of those that a mesh axis runs over, the one named last changes fastest.
Arguments:
- queries: bfloat16 [2, 4096, 1024], P('kvh', 'ctx'), may hold values from -30 to 30
- keys: bfloat16 [2, 4096, 128], P('kvh', 'ctx'), may hold values from -12 to 12
- values: bfloat16 [2, 4096, 128], P('kvh', 'ctx'), may hold values from -6 to 6
- doc_lengths: int32 [8], replicated, may hold values from 1 to 2048, 4096 in all
- w_out: bfloat16 [2048, 8192], P('kvh'), may hold values from -0.125 to 0.125
Outputs:
- layer_out: bfloat16 [4096, 8192], P(('ctx', 'kvh'))
The draws below stay inside these ranges and needn't reach their ends.
Inputs may be any that keep to these rules, and one draw needn't show every extreme that they name: `doc_lengths`: the lengths sum to 4096; the longest is exactly 2048.
All inputs are finite; a program needn't handle non-finite values.
Results may differ from the reference program's by a relative error of at most 0.013.
Values may be sent and summed in bfloat16 or wider, within the bound.
A program may use at most 192 MiB of HBM per device.

```python
import math
import jax
import jax.numpy as jnp
import numpy as np
from jax import lax

D = 8192
HD = 128
GROUP = 8
KEY_VALUE_HEADS = 2
BLOCK = 128
SPAN = 16
SEQUENCE_TOKENS = 4096
NDOCS = 8


def joint_draw(key):
    base_random_key = jax.random.fold_in(key, 9173)
    random_key_for_queries, random_key_for_keys = jax.random.split(base_random_key, 2)
    query_raw = jax.random.truncated_normal(random_key_for_queries, -6.0, 6.0, (KEY_VALUE_HEADS, SEQUENCE_TOKENS, GROUP * HD), jnp.float32)
    random_raw_input = jax.random.truncated_normal(random_key_for_keys, -6.0, 6.0, (KEY_VALUE_HEADS, SEQUENCE_TOKENS, HD), jnp.float32)
    return (query_raw, random_raw_input)


def draw_queries(key, part):
    return joint_draw(key)[0].astype(jnp.bfloat16)


def draw_keys(key, part):
    return joint_draw(key)[1].astype(jnp.bfloat16)


def block_levels(stream_key, shape, cuts, low, top_value):
    def one(axis_at, parts):
        steps = jax.random.uniform(jax.random.fold_in(jax.random.fold_in(stream_key, 6), axis_at), (parts,), jnp.float32, low / len(cuts), top_value / len(cuts))
        return jnp.repeat(jnp.exp(steps), shape[axis_at] // parts).reshape((-1,) + (1,) * (len(shape) - axis_at - 1))

    factor_of = one(*cuts[0])
    for cut in cuts[1:]:
        factor_of = factor_of * one(*cut)
    return factor_of


def profile(number_of, total, reach, lean):
    loads = [(1 << 20) // math.isqrt(standing ** lean) + 1 for standing in range(2, number_of + 1)]
    spare, holding = total - reach - (number_of - 1), [1] * (number_of - 1)
    while spare > 0:
        free = [i for i in range(number_of - 1) if holding[i] < reach]
        whole, remaining = sum([loads[i] for i in free]), spare
        for i in free:
            extra = min(reach - holding[i], max(1, remaining * loads[i] // whole), spare)
            holding[i] = holding[i] + extra
            spare = spare - extra
    return np.array([reach] + holding)


def ragged_sizes(own_key, count, total, bound, lean):
    if count == 2:
        one = jax.random.randint(own_key, (), max(1, total - bound), min(bound, total - 1) + 1)
        return jnp.stack([one, total - one])
    lengths = jnp.asarray(profile(count, total, bound, lean), jnp.int32)
    couples = (count - 1) // 2
    giver, sink = lengths[1:1 + 2 * couples:2], lengths[2:2 + 2 * couples:2]
    margin = jnp.minimum(giver - 1, bound - sink)
    moved = jax.random.randint(jax.random.fold_in(own_key, 1), (couples,), 0, 1 << 20) % (margin + 1)
    lengths = lengths.at[1:1 + 2 * couples:2].set(giver - moved).at[2:2 + 2 * couples:2].set(sink + moved)
    return lengths[jax.random.permutation(jax.random.fold_in(own_key, 2), count)]


def gaussian(key, shape, spread, limit, cuts=(), kind=jnp.bfloat16):
    array = jax.random.normal(key, shape, jnp.float32) * spread
    if len(cuts) > 0:
        array = block_levels(key, shape, cuts, -0.22, 0.18) * array
    return jnp.clip(array, min=-limit, max=limit).astype(kind)


def setup_inputs(seed: int = 0) -> dict:
    key_list = jax.random.split(jax.random.key(seed), 6)
    return {
        "queries": draw_queries(jax.random.fold_in(key_list[5], 71), 0),
        "keys": draw_keys(jax.random.fold_in(key_list[5], 71), 0),
        "values": gaussian(key_list[2], (KEY_VALUE_HEADS, SEQUENCE_TOKENS, HD), 1.0, 6.0, ((0, 2), (1, 16))),
        "doc_lengths": ragged_sizes(key_list[3], NDOCS, SEQUENCE_TOKENS, SPAN * BLOCK, 2).astype(jnp.int32),
        "w_out": gaussian(key_list[4], (KEY_VALUE_HEADS * GROUP * HD, D), (KEY_VALUE_HEADS * GROUP * HD) ** -0.5, 0.125, ((0, 2),)),
    }


NEG = -1e30


def reference(queries, keys, values, doc_lengths, w_out):
    block_total = SEQUENCE_TOKENS // BLOCK
    row_index = jnp.arange(SEQUENCE_TOKENS, dtype=jnp.int32)
    block_index = row_index // BLOCK
    holder = block_index // 2
    place = jnp.where(block_index % 2 == 0, holder, block_total - 1 - holder)
    position = (place * BLOCK + row_index % BLOCK).astype(jnp.int32)
    row_at = jnp.zeros((SEQUENCE_TOKENS,), jnp.int32).at[position].set(row_index)
    query_sorted = queries[:, row_at]
    margin_rows = SPAN * BLOCK
    keys_padded = jnp.pad(keys[:, row_at], ((0, 0), (margin_rows, 0), (0, 0)))
    values_padded = jnp.pad(values[:, row_at], ((0, 0), (margin_rows, 0), (0, 0)))
    doc_ends = jnp.cumsum(doc_lengths).astype(jnp.int32)
    span_rows = (SPAN + 1) * BLOCK
    offsets = jnp.arange(BLOCK, dtype=jnp.int32)
    window = jnp.arange(span_rows, dtype=jnp.int32)

    def one_block(block_number):
        first_pos = (block_number * BLOCK).astype(jnp.int32)
        query_block = lax.dynamic_slice_in_dim(query_sorted, first_pos, BLOCK, 1).astype(jnp.float32)
        query_block = query_block.reshape(KEY_VALUE_HEADS, BLOCK, GROUP, HD)
        key_block = lax.dynamic_slice_in_dim(keys_padded, first_pos, span_rows, 1).astype(jnp.float32)
        value_block = lax.dynamic_slice_in_dim(values_padded, first_pos, span_rows, 1).astype(jnp.float32)
        query_pos = first_pos + offsets
        key_pos = first_pos - margin_rows + window
        doc_start = jnp.sum(doc_lengths[None, :] * (doc_ends[None, :] <= query_pos[:, None]).astype(jnp.int32), axis=1)
        allowed = (key_pos[None, :] <= query_pos[:, None]) & (key_pos[None, :] >= doc_start[:, None])
        scores = jnp.einsum("gihd,gjd->ghij", query_block, key_block) * (HD ** -0.5)
        scores = jnp.where(allowed[None, None], scores, NEG)
        row_max = jnp.max(scores, axis=3, keepdims=True)
        weights = jnp.where(allowed[None, None], jnp.exp(scores - row_max), 0.0)
        denominator = jnp.sum(weights, axis=3)
        rounded = lax.optimization_barrier(weights.astype(jnp.bfloat16)).astype(jnp.float32)
        summed = jnp.einsum("ghij,gjd->gihd", rounded, value_block)
        attended = summed / jnp.transpose(denominator, (0, 2, 1))[..., None]
        return attended.astype(jnp.bfloat16).reshape(KEY_VALUE_HEADS, BLOCK, GROUP * HD)

    blocks_out = lax.map(one_block, jnp.arange(block_total, dtype=jnp.int32))
    attended_sorted = jnp.transpose(blocks_out, (1, 0, 2, 3)).reshape(KEY_VALUE_HEADS, SEQUENCE_TOKENS, GROUP * HD)
    attended_rows = attended_sorted[:, position]
    flattened = jnp.transpose(attended_rows, (1, 0, 2)).reshape(SEQUENCE_TOKENS, KEY_VALUE_HEADS * GROUP * HD)
    return jnp.dot(flattened, w_out, preferred_element_type=jnp.float32).astype(jnp.bfloat16)
```

```python
import functools
import math

import jax
import jax.numpy as jnp
from jax import lax
from jax.experimental import pallas as pl
from jax.experimental.pallas import tpu as pltpu
from jax.sharding import PartitionSpec as P

MESH = pl.DeviceIdType.MESH
NEG = -1e30
FLOOR = -1e20
COLUMNS = 512
LAG = 2


def grid_of(n):
    z = 4 if n % 4 == 0 else 1
    rest = n // z
    x = max(i for i in range(1, math.isqrt(rest) + 1) if rest % i == 0)
    return z, rest // x, x


def nearest(p, k, size):
    m = jnp.minimum(p, size - 1 - p)
    half = (k + 1) // 2
    near = jnp.where(k % 2 == 1, p + half, p - half)
    far = jnp.where(p < size - 1 - p, k, size - 1 - k)
    return jnp.where(k <= 2 * m, near, far)


def kernel(
    n,
    docs,
    lengths,
    q_hbm,
    k_ref,
    v_ref,
    w_hbm,
    out_hbm,
    kv,
    q_in,
    q_t,
    top,
    den,
    acc,
    att,
    w,
    mine,
    outgoing,
    incoming,
    result,
    local_sem,
    send_sem,
    recv_sem,
    part_send,
    part_recv,
    out_sem,
):
    sizes = grid_of(n)
    Z, Y, X = sizes
    block = k_ref.shape[1] // 2
    hd = k_ref.shape[2]
    width = q_in.shape[1]
    heads = width // hd
    me = lax.axis_index("ctx")
    core = lax.axis_index("kvh")
    place = (me // (Y * X), (me // X) % Y, me % X)
    strides = (Y * X, X, 1)

    q_copy = pltpu.make_async_copy(q_hbm.at[0], q_in, local_sem.at[0])
    q_copy.start()
    w_copy = pltpu.make_async_copy(w_hbm, w, local_sem.at[1])

    barrier = pltpu.get_barrier_semaphore()
    count = jnp.int32(1)
    pl.semaphore_signal(
        barrier, inc=1, device_id={"kvh": 1 - core}, device_id_type=MESH
    )
    for axis in range(3):
        for step in (1, -1):
            there = place[axis] + step
            exists = (there >= 0) & (there < sizes[axis])
            count = count + exists.astype(jnp.int32)

            @pl.when(exists)
            def _(axis=axis, step=step):
                pl.semaphore_signal(
                    barrier,
                    inc=1,
                    device_id={"ctx": me + step * strides[axis]},
                    device_id_type=MESH,
                )

    for b in range(2):
        kv[me, b, 0:block] = k_ref[0, b * block : (b + 1) * block]
        kv[me, b, block:] = v_ref[0, b * block : (b + 1) * block].T
    pl.semaphore_wait(barrier, count)

    def wanted(b, source, low, high):
        if b == 0:
            return high >= jnp.minimum(source, n - 1 - source)
        return low <= source

    def index(coords):
        return sum(c * s for c, s in zip(coords, strides))

    def tree(source, b):
        order = (0, 2, 1) if b == 0 else (0, 1, 2)
        src = (source // (Y * X), (source // X) % Y, source % X)
        edges = []
        arrives = jnp.bool_(False)
        on_line = jnp.bool_(True)
        for depth in (2, 1, 0):
            axis = order[depth]
            inner = order[depth + 1 :]
            p, s = place[axis], src[axis]
            first, last = list(place), list(place)
            for a in inner:
                first[a], last[a] = 0, sizes[a] - 1
            for step in (1, -1):
                there = p + step
                first_a, last_a = (there, sizes[axis] - 1) if step == 1 else (0, there)
                first[axis], last[axis] = first_a, last_a
                exists = (there >= 0) & (there < sizes[axis])
                onward = (p >= s) if step == 1 else (p <= s)
                go = on_line & exists & onward
                go = go & wanted(b, source, index(first), index(last))
                edges.append((go, axis * 2 + (step == 1), me + step * strides[axis]))
                first[axis], last[axis] = (p, sizes[axis] - 1) if step == 1 else (0, p)
                passed = (p > s) if step == 1 else (p < s)
                arrives = arrives | (
                    on_line & passed & wanted(b, source, index(first), index(last))
                )
            on_line = on_line & (p == s)
        return edges, arrives

    def copy_of(source, b, way, target):
        return pltpu.make_async_remote_copy(
            src_ref=kv.at[source, b],
            dst_ref=kv.at[source, b],
            send_sem=send_sem.at[source, b, way],
            recv_sem=recv_sem.at[source, b],
            device_id={"ctx": target},
            device_id_type=MESH,
        )

    def pass_on(source):
        for b in range(2):
            edges, arrives = tree(source, b)

            @pl.when(arrives)
            def _(b=b):
                copy_of(source, b, 0, me).wait_recv()

            for go, way, target in reversed(edges):

                @pl.when(go)
                def _(b=b, way=way, target=target):
                    copy_of(source, b, way, target).start()

    pass_on(me)
    w_copy.start()

    q_copy.wait()
    for b in range(2):
        for h in range(heads):
            q_t[b, :, h * hd : (h + 1) * hd] = q_in[
                b * block : (b + 1) * block, h * hd : (h + 1) * hd
            ].T
    top[...] = jnp.full(top.shape, FLOOR, jnp.float32)
    den[...] = jnp.zeros(den.shape, jnp.float32)
    acc[...] = jnp.zeros(acc.shape, jnp.float32)

    own_blocks = (me, 2 * n - 1 - me)
    lanes = lax.broadcasted_iota(jnp.int32, (1, block), 1)
    query_pos = [c * block + lanes for c in own_blocks]
    doc_start = [jnp.zeros((1, block), jnp.int32) for _ in own_blocks]
    end = jnp.int32(0)
    for i in range(docs):
        length = lengths[i]
        end = end + length
        doc_start = [
            s + jnp.where(end <= p, length, 0) for s, p in zip(doc_start, query_pos)
        ]

    factor = hd ** (-0.5) * math.log2(math.e)
    rows = lax.broadcasted_iota(jnp.int32, (block, block), 0)
    group = 2 * hd if heads % 2 == 0 else hd

    def absorb(qb, source, blocks):
        biases, keys, vals = [], [], []
        for b in blocks:
            c = source if b == 0 else 2 * n - 1 - source
            key_pos = c * block + rows
            allowed = (key_pos <= query_pos[qb]) & (key_pos >= doc_start[qb])
            biases.append(jnp.where(allowed, 0.0, NEG))
            keys.append(kv[source, b, 0:block])
            vals.append(kv[source, b, block:])
        bias = jnp.concatenate(biases, axis=0) if len(blocks) > 1 else biases[0]
        bias = jnp.concatenate([bias] * (group // block), axis=1)
        key = jnp.concatenate(keys, axis=0) if len(blocks) > 1 else keys[0]
        val = jnp.concatenate(vals, axis=1) if len(blocks) > 1 else vals[0]
        for c in range(width // group):
            cols = slice(c * group, (c + 1) * group)
            scores = jnp.dot(key, q_t[qb, :, cols], preferred_element_type=jnp.float32)
            scores = scores + bias
            old = top[qb, :, cols]
            new = jnp.maximum(old, jnp.max(scores, axis=0, keepdims=True))
            weights = jnp.exp2((scores - new) * factor)
            rescale = jnp.exp2((old - new) * factor)
            top[qb, :, cols] = new
            den[qb, :, cols] = den[qb, :, cols] * rescale + jnp.sum(
                weights, axis=0, keepdims=True
            )
            acc[qb, :, cols] = acc[qb, :, cols] * rescale + jnp.dot(
                val, weights.astype(jnp.bfloat16), preferred_element_type=jnp.float32
            )

    plane = Y * X

    def source_at(kz, j):
        return index(
            (
                nearest(place[0], kz, Z),
                nearest(place[1], j // X, Y),
                nearest(place[2], j % X, X),
            )
        )

    def visit(r, carry):
        kz, j = r // plane, r % plane
        source = source_at(kz, j)

        @pl.when((j == 0) & (kz + 1 < Z))
        def _():
            pass_on(source_at(kz + 1, 0))

        @pl.when(j > 0)
        def _():
            pass_on(source)

        low = source >= n - 1 - me
        high = source >= me

        @pl.when(source <= me)
        def _():
            absorb(0, source, (0,))

        @pl.when(low & high)
        def _():
            absorb(1, source, (0, 1))

        @pl.when(low & jnp.logical_not(high))
        def _():
            absorb(1, source, (0,))

        @pl.when(high & jnp.logical_not(low))
        def _():
            absorb(1, source, (1,))

        return carry

    lax.fori_loop(0, n, visit, 0)

    for qb in range(2):
        spot = (1 - core) if qb == 0 else core
        at = pl.multiple_of(spot * block, block)
        for h in range(heads):
            cols = slice(h * hd, (h + 1) * hd)
            o = acc[qb, :, cols] / den[qb, :, cols]
            att[pl.ds(at, block), cols] = o.T.astype(jnp.bfloat16)

    w_copy.wait()
    chunks = w.shape[1] // COLUMNS

    def part(j):
        return pltpu.make_async_remote_copy(
            src_ref=outgoing.at[j],
            dst_ref=incoming.at[j],
            send_sem=part_send.at[j],
            recv_sem=part_recv.at[j],
            device_id={"kvh": 1 - core},
            device_id_type=MESH,
        )

    def store(j):
        at = pl.multiple_of(j * COLUMNS, COLUMNS)
        return pltpu.make_async_copy(
            result.at[j], out_hbm.at[:, pl.ds(at, COLUMNS)], out_sem.at[j]
        )

    def finish(j):
        part(j).wait_recv()
        total = mine[j] + incoming[j].astype(jnp.float32)
        result[j] = total.astype(jnp.bfloat16)
        store(j).start()

    def project(j, carry):
        at = pl.multiple_of(j * COLUMNS, COLUMNS)
        both = jnp.dot(
            att[...], w[:, pl.ds(at, COLUMNS)], preferred_element_type=jnp.float32
        )
        outgoing[j] = both[:block].astype(jnp.bfloat16)
        part(j).start()
        mine[j] = both[block:]

        @pl.when(j >= LAG)
        def _():
            finish(j - LAG)

        return carry

    lax.fori_loop(0, chunks, project, 0)

    def tail(j, carry):
        finish(j)
        return carry

    lax.fori_loop(chunks - LAG, chunks, tail, 0)

    def sent(source, carry):
        for b in range(2):
            for go, way, target in tree(source, b)[0]:

                @pl.when(go)
                def _(b=b, way=way, target=target):
                    copy_of(source, b, way, target).wait_send()

        return carry

    lax.fori_loop(0, n, sent, 0)

    def stored(j, carry):
        part(j).wait_send()
        store(j).wait()
        return carry

    lax.fori_loop(0, chunks, stored, 0)


def on_device(n, queries, keys, values, doc_lengths, w_out):
    rows, hd = keys.shape[1:]
    width = queries.shape[2]
    block = rows // 2
    model = w_out.shape[1]
    chunks = model // COLUMNS
    vmem = pl.BlockSpec(memory_space=pltpu.VMEM)
    far = pl.BlockSpec(memory_space=pl.ANY)
    pairs = 2 * n + 2
    return pl.pallas_call(
        functools.partial(kernel, n, doc_lengths.shape[0]),
        out_shape=jax.ShapeDtypeStruct((block, model), jnp.bfloat16),
        in_specs=[pl.BlockSpec(memory_space=pltpu.SMEM), far, vmem, vmem, far],
        out_specs=far,
        scratch_shapes=[
            pltpu.VMEM((n, 2, 2 * block, hd), jnp.bfloat16),
            pltpu.VMEM((rows, width), jnp.bfloat16),
            pltpu.VMEM((2, hd, width), jnp.bfloat16),
            pltpu.VMEM((2, 1, width), jnp.float32),
            pltpu.VMEM((2, 1, width), jnp.float32),
            pltpu.VMEM((2, hd, width), jnp.float32),
            pltpu.VMEM((rows, width), jnp.bfloat16),
            pltpu.VMEM(w_out.shape, jnp.bfloat16),
            pltpu.VMEM((chunks, block, COLUMNS), jnp.float32),
            pltpu.VMEM((chunks, block, COLUMNS), jnp.bfloat16),
            pltpu.VMEM((chunks, block, COLUMNS), jnp.bfloat16),
            pltpu.VMEM((chunks, block, COLUMNS), jnp.bfloat16),
            pltpu.SemaphoreType.DMA((2,)),
            pltpu.SemaphoreType.DMA((n, 2, 6)),
            pltpu.SemaphoreType.DMA((n, 2)),
            pltpu.SemaphoreType.DMA((chunks,)),
            pltpu.SemaphoreType.DMA((chunks,)),
            pltpu.SemaphoreType.DMA((chunks,)),
        ],
        compiler_params=pltpu.CompilerParams(
            collective_id=0, has_side_effects=True, vmem_limit_bytes=56 * 1024 * 1024
        ),
        cost_estimate=pl.CostEstimate(
            flops=4 * pairs * block * block * width + 2 * rows * width * model,
            bytes_accessed=2 * (w_out.size + block * model),
            transcendentals=pairs * block * width,
        ),
        name="attend_and_project",
    )(doc_lengths, queries, keys, values, w_out)


def solution(mesh):
    in_specs = (
        P("kvh", "ctx", None),
        P("kvh", "ctx", None),
        P("kvh", "ctx", None),
        P(),
        P("kvh", None),
    )
    out_specs = P(("ctx", "kvh"), None)
    return jax.shard_map(
        functools.partial(on_device, mesh.shape["ctx"]),
        mesh=mesh,
        in_specs=in_specs,
        out_specs=out_specs,
        check_vma=False,
    )
```

```python
import functools
import math

import jax
import jax.numpy as jnp
from jax import lax
from jax.experimental import pallas as pl
from jax.experimental.pallas import tpu as pltpu
from jax.sharding import PartitionSpec as P

MESH = pl.DeviceIdType.MESH
NEG = -1e30
FLOOR = -1e20
COLUMNS = 512
LAG = 2


def grid_of(n):
    z = 4 if n % 4 == 0 else 1
    rest = n // z
    x = max(i for i in range(1, math.isqrt(rest) + 1) if rest % i == 0)
    return z, rest // x, x


def nearest(p, k, size):
    m = jnp.minimum(p, size - 1 - p)
    half = (k + 1) // 2
    near = jnp.where(k % 2 == 1, p + half, p - half)
    far = jnp.where(p < size - 1 - p, k, size - 1 - k)
    return jnp.where(k <= 2 * m, near, far)


def kernel(
    n,
    docs,
    lengths,
    q_hbm,
    k_ref,
    v_ref,
    w_hbm,
    out_hbm,
    kv,
    q_in,
    q_t,
    top,
    den,
    acc,
    att,
    w,
    mine,
    outgoing,
    incoming,
    result,
    local_sem,
    send_sem,
    recv_sem,
    part_send,
    part_recv,
    out_sem,
):
    sizes = grid_of(n)
    Z, Y, X = sizes
    block = k_ref.shape[1] // 2
    hd = k_ref.shape[2]
    width = q_in.shape[1]
    heads = width // hd
    me = lax.axis_index("ctx")
    core = lax.axis_index("kvh")
    place = (me // (Y * X), (me // X) % Y, me % X)
    strides = (Y * X, X, 1)

    q_copy = pltpu.make_async_copy(q_hbm.at[0], q_in, local_sem.at[0])
    q_copy.start()
    w_copy = pltpu.make_async_copy(w_hbm, w, local_sem.at[1])

    barrier = pltpu.get_barrier_semaphore()
    count = jnp.int32(1)
    pl.semaphore_signal(
        barrier, inc=1, device_id={"kvh": 1 - core}, device_id_type=MESH
    )
    for axis in range(3):
        for step in (1, -1):
            there = place[axis] + step
            exists = (there >= 0) & (there < sizes[axis])
            count = count + exists.astype(jnp.int32)

            @pl.when(exists)
            def _(axis=axis, step=step):
                pl.semaphore_signal(
                    barrier,
                    inc=1,
                    device_id={"ctx": me + step * strides[axis]},
                    device_id_type=MESH,
                )

    for b in range(2):
        kv[me, b, 0:block] = k_ref[0, b * block : (b + 1) * block]
        kv[me, b, block:] = v_ref[0, b * block : (b + 1) * block].T
    pl.semaphore_wait(barrier, count)

    def wanted(b, source, low, high):
        pair = source // 2
        if b == 0:
            return high >= jnp.minimum(2 * pair, n - 2 - 2 * pair)
        return low <= 2 * pair + 1

    def index(coords):
        return sum(c * s for c, s in zip(coords, strides))

    def tree(source, b):
        order = (0, 2, 1) if b == 0 else (0, 1, 2)
        src = (source // (Y * X), (source // X) % Y, source % X)
        edges = []
        arrives = jnp.bool_(False)
        on_line = jnp.bool_(True)
        for depth in (2, 1, 0):
            axis = order[depth]
            inner = order[depth + 1 :]
            p, s = place[axis], src[axis]
            first, last = list(place), list(place)
            for a in inner:
                first[a], last[a] = 0, sizes[a] - 1
            for step in (1, -1):
                there = p + step
                first_a, last_a = (there, sizes[axis] - 1) if step == 1 else (0, there)
                first[axis], last[axis] = first_a, last_a
                exists = (there >= 0) & (there < sizes[axis])
                onward = (p >= s) if step == 1 else (p <= s)
                go = on_line & exists & onward
                go = go & wanted(b, source, index(first), index(last))
                edges.append((go, axis * 2 + (step == 1), me + step * strides[axis]))
                first[axis], last[axis] = (p, sizes[axis] - 1) if step == 1 else (0, p)
                passed = (p > s) if step == 1 else (p < s)
                arrives = arrives | (
                    on_line & passed & wanted(b, source, index(first), index(last))
                )
            on_line = on_line & (p == s)
        return edges, arrives

    def copy_of(source, b, way, target):
        return pltpu.make_async_remote_copy(
            src_ref=kv.at[source, b],
            dst_ref=kv.at[source, b],
            send_sem=send_sem.at[source, b, way],
            recv_sem=recv_sem.at[source, b],
            device_id={"ctx": target},
            device_id_type=MESH,
        )

    def pass_on(source):
        for b in range(2):
            edges, arrives = tree(source, b)

            @pl.when(arrives)
            def _(b=b):
                copy_of(source, b, 0, me).wait_recv()

            for go, way, target in reversed(edges):

                @pl.when(go)
                def _(b=b, way=way, target=target):
                    copy_of(source, b, way, target).start()

    pass_on(me)
    w_copy.start()

    q_copy.wait()
    for b in range(2):
        for h in range(heads):
            q_t[b, :, h * hd : (h + 1) * hd] = q_in[
                b * block : (b + 1) * block, h * hd : (h + 1) * hd
            ].T
    top[...] = jnp.full(top.shape, FLOOR, jnp.float32)
    den[...] = jnp.zeros(den.shape, jnp.float32)
    acc[...] = jnp.zeros(acc.shape, jnp.float32)

    own_blocks = (me, 2 * n - 1 - me)
    lanes = lax.broadcasted_iota(jnp.int32, (1, block), 1)
    query_pos = [c * block + lanes for c in own_blocks]
    doc_start = [jnp.zeros((1, block), jnp.int32) for _ in own_blocks]
    end = jnp.int32(0)
    for i in range(docs):
        length = lengths[i]
        end = end + length
        doc_start = [
            s + jnp.where(end <= p, length, 0) for s, p in zip(doc_start, query_pos)
        ]

    factor = hd ** (-0.5) * math.log2(math.e)
    rows = lax.broadcasted_iota(jnp.int32, (block, block), 0)
    group = 2 * hd if heads % 2 == 0 else hd

    def absorb(qb, pair, b):
        biases, keys, vals = [], [], []
        for source in (2 * pair, 2 * pair + 1):
            c = source if b == 0 else 2 * n - 1 - source
            key_pos = c * block + rows
            allowed = (key_pos <= query_pos[qb]) & (key_pos >= doc_start[qb])
            biases.append(jnp.where(allowed, 0.0, NEG))
            keys.append(kv[source, b, 0:block])
            vals.append(kv[source, b, block:])
        bias = jnp.concatenate(biases, axis=0)
        bias = jnp.concatenate([bias] * (group // block), axis=1)
        key = jnp.concatenate(keys, axis=0)
        val = jnp.concatenate(vals, axis=1)
        for c in range(width // group):
            cols = slice(c * group, (c + 1) * group)
            scores = jnp.dot(key, q_t[qb, :, cols], preferred_element_type=jnp.float32)
            scores = scores + bias
            old = top[qb, :, cols]
            new = jnp.maximum(old, jnp.max(scores, axis=0, keepdims=True))
            weights = jnp.exp2((scores - new) * factor)
            rescale = jnp.exp2((old - new) * factor)
            top[qb, :, cols] = new
            den[qb, :, cols] = den[qb, :, cols] * rescale + jnp.sum(
                weights, axis=0, keepdims=True
            )
            acc[qb, :, cols] = acc[qb, :, cols] * rescale + jnp.dot(
                val, weights.astype(jnp.bfloat16), preferred_element_type=jnp.float32
            )

    plane = Y * X

    def source_at(kz, j):
        x, kx = place[2], j % X
        return index(
            (
                nearest(place[0], kz, Z),
                nearest(place[1], j // X, Y),
                nearest(x // 2, kx // 2, X // 2) * 2 + (x + kx) % 2,
            )
        )

    def visit(r, carry):
        kz, j = r // (plane // 2), 2 * (r % (plane // 2))
        source = source_at(kz, j)

        @pl.when((j == 0) & (kz + 1 < Z))
        def _():
            pass_on(source_at(kz + 1, 0))

        @pl.when(j > 0)
        def _():
            pass_on(source)

        pass_on(source_at(kz, j + 1))
        pair = source // 2

        @pl.when(2 * pair <= me)
        def _():
            absorb(0, pair, 0)

        @pl.when(2 * pair + 1 >= n - 1 - me)
        def _():
            absorb(1, pair, 0)

        @pl.when(2 * pair + 1 >= me)
        def _():
            absorb(1, pair, 1)

        return carry

    lax.fori_loop(0, n // 2, visit, 0)

    for qb in range(2):
        spot = (1 - core) if qb == 0 else core
        at = pl.multiple_of(spot * block, block)
        for h in range(heads):
            cols = slice(h * hd, (h + 1) * hd)
            o = acc[qb, :, cols] / den[qb, :, cols]
            att[pl.ds(at, block), cols] = o.T.astype(jnp.bfloat16)

    w_copy.wait()
    chunks = w.shape[1] // COLUMNS

    def part(j):
        return pltpu.make_async_remote_copy(
            src_ref=outgoing.at[j],
            dst_ref=incoming.at[j],
            send_sem=part_send.at[j],
            recv_sem=part_recv.at[j],
            device_id={"kvh": 1 - core},
            device_id_type=MESH,
        )

    def store(j):
        at = pl.multiple_of(j * COLUMNS, COLUMNS)
        return pltpu.make_async_copy(
            result.at[j], out_hbm.at[:, pl.ds(at, COLUMNS)], out_sem.at[j]
        )

    def finish(j):
        part(j).wait_recv()
        total = mine[j] + incoming[j].astype(jnp.float32)
        result[j] = total.astype(jnp.bfloat16)
        store(j).start()

    def project(j, carry):
        at = pl.multiple_of(j * COLUMNS, COLUMNS)
        both = jnp.dot(
            att[...], w[:, pl.ds(at, COLUMNS)], preferred_element_type=jnp.float32
        )
        outgoing[j] = both[:block].astype(jnp.bfloat16)
        part(j).start()
        mine[j] = both[block:]

        @pl.when(j >= LAG)
        def _():
            finish(j - LAG)

        return carry

    lax.fori_loop(0, chunks, project, 0)

    def tail(j, carry):
        finish(j)
        return carry

    lax.fori_loop(chunks - LAG, chunks, tail, 0)

    def sent(source, carry):
        for b in range(2):
            for go, way, target in tree(source, b)[0]:

                @pl.when(go)
                def _(b=b, way=way, target=target):
                    copy_of(source, b, way, target).wait_send()

        return carry

    lax.fori_loop(0, n, sent, 0)

    def stored(j, carry):
        part(j).wait_send()
        store(j).wait()
        return carry

    lax.fori_loop(0, chunks, stored, 0)


def on_device(n, queries, keys, values, doc_lengths, w_out):
    rows, hd = keys.shape[1:]
    width = queries.shape[2]
    block = rows // 2
    model = w_out.shape[1]
    chunks = model // COLUMNS
    vmem = pl.BlockSpec(memory_space=pltpu.VMEM)
    far = pl.BlockSpec(memory_space=pl.ANY)
    pairs = 2 * n + 2
    return pl.pallas_call(
        functools.partial(kernel, n, doc_lengths.shape[0]),
        out_shape=jax.ShapeDtypeStruct((block, model), jnp.bfloat16),
        in_specs=[pl.BlockSpec(memory_space=pltpu.SMEM), far, vmem, vmem, far],
        out_specs=far,
        scratch_shapes=[
            pltpu.VMEM((n, 2, 2 * block, hd), jnp.bfloat16),
            pltpu.VMEM((rows, width), jnp.bfloat16),
            pltpu.VMEM((2, hd, width), jnp.bfloat16),
            pltpu.VMEM((2, 1, width), jnp.float32),
            pltpu.VMEM((2, 1, width), jnp.float32),
            pltpu.VMEM((2, hd, width), jnp.float32),
            pltpu.VMEM((rows, width), jnp.bfloat16),
            pltpu.VMEM(w_out.shape, jnp.bfloat16),
            pltpu.VMEM((chunks, block, COLUMNS), jnp.float32),
            pltpu.VMEM((chunks, block, COLUMNS), jnp.bfloat16),
            pltpu.VMEM((chunks, block, COLUMNS), jnp.bfloat16),
            pltpu.VMEM((chunks, block, COLUMNS), jnp.bfloat16),
            pltpu.SemaphoreType.DMA((2,)),
            pltpu.SemaphoreType.DMA((n, 2, 6)),
            pltpu.SemaphoreType.DMA((n, 2)),
            pltpu.SemaphoreType.DMA((chunks,)),
            pltpu.SemaphoreType.DMA((chunks,)),
            pltpu.SemaphoreType.DMA((chunks,)),
        ],
        compiler_params=pltpu.CompilerParams(
            collective_id=0, has_side_effects=True, vmem_limit_bytes=56 * 1024 * 1024
        ),
        cost_estimate=pl.CostEstimate(
            flops=4 * pairs * block * block * width + 2 * rows * width * model,
            bytes_accessed=2 * (w_out.size + block * model),
            transcendentals=pairs * block * width,
        ),
        name="attend_and_project",
    )(doc_lengths, queries, keys, values, w_out)


def solution(mesh):
    in_specs = (
        P("kvh", "ctx", None),
        P("kvh", "ctx", None),
        P("kvh", "ctx", None),
        P(),
        P("kvh", None),
    )
    out_specs = P(("ctx", "kvh"), None)
    return jax.shard_map(
        functools.partial(on_device, mesh.shape["ctx"]),
        mesh=mesh,
        in_specs=in_specs,
        out_specs=out_specs,
        check_vma=False,
    )
```

```python
import functools
import math

import jax
import jax.numpy as jnp
from jax import lax
from jax.experimental import pallas as pl
from jax.experimental.pallas import tpu as pltpu
from jax.sharding import PartitionSpec as P

MESH = pl.DeviceIdType.MESH
NEG = -1e30
FLOOR = -1e20
COLUMNS = 2048
LAG = 2


def grid_of(n):
    z = 4 if n % 4 == 0 else 1
    rest = n // z
    x = max(i for i in range(1, math.isqrt(rest) + 1) if rest % i == 0)
    return z, rest // x, x


def div(a, k):
    return a >> (k.bit_length() - 1) if k & (k - 1) == 0 else a // k


def mod(a, k):
    return a & (k - 1) if k & (k - 1) == 0 else a % k


def nearest(p, k, size):
    m = jnp.minimum(p, size - 1 - p)
    half = div(k + 1, 2)
    near = jnp.where(mod(k, 2) == 1, p + half, p - half)
    far = jnp.where(p < size - 1 - p, k, size - 1 - k)
    return jnp.where(k <= 2 * m, near, far)


def kernel(
    n,
    docs,
    lengths,
    q_hbm,
    k_ref,
    v_ref,
    w_hbm,
    out_hbm,
    kv,
    q_in,
    q_t,
    top,
    den,
    acc,
    att,
    w,
    mine,
    outgoing,
    incoming,
    result,
    local_sem,
    send_sem,
    recv_sem,
    part_send,
    part_recv,
    out_sem,
):
    sizes = grid_of(n)
    Z, Y, X = sizes
    block = k_ref.shape[1] // 2
    hd = k_ref.shape[2]
    width = q_in.shape[1]
    heads = width // hd
    me = lax.axis_index("ctx")
    core = lax.axis_index("kvh")
    place = (div(me, Y * X), mod(div(me, X), Y), mod(me, X))
    strides = (Y * X, X, 1)

    q_copy = pltpu.make_async_copy(q_hbm.at[0], q_in, local_sem.at[0])
    q_copy.start()
    w_copy = pltpu.make_async_copy(w_hbm, w, local_sem.at[1])

    barrier = pltpu.get_barrier_semaphore()
    count = jnp.int32(1)
    pl.semaphore_signal(
        barrier, inc=1, device_id={"kvh": 1 - core}, device_id_type=MESH
    )
    for axis in range(3):
        for step in (1, -1):
            there = place[axis] + step
            exists = (there >= 0) & (there < sizes[axis])
            count = count + exists.astype(jnp.int32)

            @pl.when(exists)
            def _(axis=axis, step=step):
                pl.semaphore_signal(
                    barrier,
                    inc=1,
                    device_id={"ctx": me + step * strides[axis]},
                    device_id_type=MESH,
                )

    for b in range(2):
        kv[me, b, 0:block] = k_ref[0, b * block : (b + 1) * block]
        kv[me, b, block:] = v_ref[0, b * block : (b + 1) * block].T
    pl.semaphore_wait(barrier, count)

    def wanted(b, source, low, high):
        if b == 0:
            return high >= jnp.minimum(source, n - 1 - source)
        return low <= source

    def index(coords):
        return sum(c * s for c, s in zip(coords, strides))

    def tree(source, b):
        order = (0, 2, 1) if b == 0 else (0, 1, 2)
        src = (div(source, Y * X), mod(div(source, X), Y), mod(source, X))
        edges = []
        arrives = jnp.bool_(False)
        on_line = jnp.bool_(True)
        for depth in (2, 1, 0):
            axis = order[depth]
            inner = order[depth + 1 :]
            p, s = place[axis], src[axis]
            first, last = list(place), list(place)
            for a in inner:
                first[a], last[a] = 0, sizes[a] - 1
            for step in (1, -1):
                there = p + step
                first_a, last_a = (there, sizes[axis] - 1) if step == 1 else (0, there)
                first[axis], last[axis] = first_a, last_a
                exists = (there >= 0) & (there < sizes[axis])
                onward = (p >= s) if step == 1 else (p <= s)
                go = on_line & exists & onward
                go = go & wanted(b, source, index(first), index(last))
                edges.append((go, axis * 2 + (step == 1), me + step * strides[axis]))
                first[axis], last[axis] = (p, sizes[axis] - 1) if step == 1 else (0, p)
                passed = (p > s) if step == 1 else (p < s)
                arrives = arrives | (
                    on_line & passed & wanted(b, source, index(first), index(last))
                )
            on_line = on_line & (p == s)
        return edges, arrives

    def copy_of(source, b, way, target):
        return pltpu.make_async_remote_copy(
            src_ref=kv.at[source, b],
            dst_ref=kv.at[source, b],
            send_sem=send_sem.at[source, b, way],
            recv_sem=recv_sem.at[source, b],
            device_id={"ctx": target},
            device_id_type=MESH,
        )

    def pass_on(source):
        for b in range(2):
            edges, arrives = tree(source, b)

            @pl.when(arrives)
            def _(b=b):
                copy_of(source, b, 0, me).wait_recv()

            for go, way, target in reversed(edges):

                @pl.when(go)
                def _(b=b, way=way, target=target):
                    copy_of(source, b, way, target).start()

    pass_on(me)
    w_copy.start()

    q_copy.wait()
    for b in range(2):
        for h in range(heads):
            q_t[b, :, h * hd : (h + 1) * hd] = q_in[
                b * block : (b + 1) * block, h * hd : (h + 1) * hd
            ].T
    top[...] = jnp.full(top.shape, FLOOR, jnp.float32)
    den[...] = jnp.zeros(den.shape, jnp.float32)
    acc[...] = jnp.zeros(acc.shape, jnp.float32)

    own_blocks = (me, 2 * n - 1 - me)
    lanes = lax.broadcasted_iota(jnp.int32, (1, block), 1)
    query_pos = [c * block + lanes for c in own_blocks]
    doc_start = [jnp.zeros((1, block), jnp.int32) for _ in own_blocks]
    end = jnp.int32(0)
    for i in range(docs):
        length = lengths[i]
        end = end + length
        doc_start = [
            s + jnp.where(end <= p, length, 0) for s, p in zip(doc_start, query_pos)
        ]

    factor = hd ** (-0.5) * math.log2(math.e)
    rows = lax.broadcasted_iota(jnp.int32, (block, block), 0)
    group = 2 * hd if heads % 2 == 0 else hd

    def absorb(qb, source, blocks):
        biases, keys, vals = [], [], []
        for b in blocks:
            c = source if b == 0 else 2 * n - 1 - source
            key_pos = c * block + rows
            allowed = (key_pos <= query_pos[qb]) & (key_pos >= doc_start[qb])
            biases.append(jnp.where(allowed, 0.0, NEG))
            keys.append(kv[source, b, 0:block])
            vals.append(kv[source, b, block:])
        bias = jnp.concatenate(biases, axis=0) if len(blocks) > 1 else biases[0]
        bias = jnp.concatenate([bias] * (group // block), axis=1)
        key = jnp.concatenate(keys, axis=0) if len(blocks) > 1 else keys[0]
        val = jnp.concatenate(vals, axis=1) if len(blocks) > 1 else vals[0]
        for c in range(width // group):
            cols = slice(c * group, (c + 1) * group)
            scores = jnp.dot(key, q_t[qb, :, cols], preferred_element_type=jnp.float32)
            scores = scores + bias
            old = top[qb, :, cols]
            new = jnp.maximum(old, jnp.max(scores, axis=0, keepdims=True))
            weights = jnp.exp2((scores - new) * factor)
            rescale = jnp.exp2((old - new) * factor)
            top[qb, :, cols] = new
            den[qb, :, cols] = den[qb, :, cols] * rescale + jnp.sum(
                weights, axis=0, keepdims=True
            )
            acc[qb, :, cols] = acc[qb, :, cols] * rescale + jnp.dot(
                val, weights.astype(jnp.bfloat16), preferred_element_type=jnp.float32
            )

    plane = Y * X

    def source_at(kz, j):
        return index(
            (
                nearest(place[0], kz, Z),
                nearest(place[1], div(j, X), Y),
                nearest(place[2], mod(j, X), X),
            )
        )

    def visit(r, carry):
        kz, j = div(r, plane), mod(r, plane)
        source = source_at(kz, j)

        @pl.when((j == 0) & (kz + 1 < Z))
        def _():
            pass_on(source_at(kz + 1, 0))

        @pl.when(j > 0)
        def _():
            pass_on(source)

        low = source >= n - 1 - me
        high = source >= me

        @pl.when(source <= me)
        def _():
            absorb(0, source, (0,))

        @pl.when(low & high)
        def _():
            absorb(1, source, (0, 1))

        @pl.when(low & jnp.logical_not(high))
        def _():
            absorb(1, source, (0,))

        @pl.when(high & jnp.logical_not(low))
        def _():
            absorb(1, source, (1,))

        return carry

    lax.fori_loop(0, n, visit, 0)

    for qb in range(2):
        spot = (1 - core) if qb == 0 else core
        at = pl.multiple_of(spot * block, block)
        for h in range(heads):
            cols = slice(h * hd, (h + 1) * hd)
            o = acc[qb, :, cols] / den[qb, :, cols]
            att[pl.ds(at, block), cols] = o.T.astype(jnp.bfloat16)

    w_copy.wait()
    chunks = w.shape[1] // COLUMNS

    def part(j):
        return pltpu.make_async_remote_copy(
            src_ref=outgoing.at[j],
            dst_ref=incoming.at[j],
            send_sem=part_send.at[j],
            recv_sem=part_recv.at[j],
            device_id={"kvh": 1 - core},
            device_id_type=MESH,
        )

    def store(j):
        at = pl.multiple_of(j * COLUMNS, COLUMNS)
        return pltpu.make_async_copy(
            result.at[j], out_hbm.at[:, pl.ds(at, COLUMNS)], out_sem.at[j]
        )

    def finish(j):
        part(j).wait_recv()
        total = mine[j] + incoming[j].astype(jnp.float32)
        result[j] = total.astype(jnp.bfloat16)
        store(j).start()

    def project(j, carry):
        at = pl.multiple_of(j * COLUMNS, COLUMNS)
        both = jnp.dot(
            att[...], w[:, pl.ds(at, COLUMNS)], preferred_element_type=jnp.float32
        )
        outgoing[j] = both[:block].astype(jnp.bfloat16)
        part(j).start()
        mine[j] = both[block:]

        @pl.when(j >= LAG)
        def _():
            finish(j - LAG)

        return carry

    lax.fori_loop(0, chunks, project, 0)

    def tail(j, carry):
        finish(j)
        return carry

    lax.fori_loop(chunks - LAG, chunks, tail, 0)

    def sent(source, carry):
        for b in range(2):
            for go, way, target in tree(source, b)[0]:

                @pl.when(go)
                def _(b=b, way=way, target=target):
                    copy_of(source, b, way, target).wait_send()

        return carry

    lax.fori_loop(0, n, sent, 0)

    def stored(j, carry):
        part(j).wait_send()
        store(j).wait()
        return carry

    lax.fori_loop(0, chunks, stored, 0)


def on_device(n, queries, keys, values, doc_lengths, w_out):
    rows, hd = keys.shape[1:]
    width = queries.shape[2]
    block = rows // 2
    model = w_out.shape[1]
    chunks = model // COLUMNS
    vmem = pl.BlockSpec(memory_space=pltpu.VMEM)
    far = pl.BlockSpec(memory_space=pl.ANY)
    pairs = 2 * n + 2
    return pl.pallas_call(
        functools.partial(kernel, n, doc_lengths.shape[0]),
        out_shape=jax.ShapeDtypeStruct((block, model), jnp.bfloat16),
        in_specs=[pl.BlockSpec(memory_space=pltpu.SMEM), far, vmem, vmem, far],
        out_specs=far,
        scratch_shapes=[
            pltpu.VMEM((n, 2, 2 * block, hd), jnp.bfloat16),
            pltpu.VMEM((rows, width), jnp.bfloat16),
            pltpu.VMEM((2, hd, width), jnp.bfloat16),
            pltpu.VMEM((2, 1, width), jnp.float32),
            pltpu.VMEM((2, 1, width), jnp.float32),
            pltpu.VMEM((2, hd, width), jnp.float32),
            pltpu.VMEM((rows, width), jnp.bfloat16),
            pltpu.VMEM(w_out.shape, jnp.bfloat16),
            pltpu.VMEM((chunks, block, COLUMNS), jnp.float32),
            pltpu.VMEM((chunks, block, COLUMNS), jnp.bfloat16),
            pltpu.VMEM((chunks, block, COLUMNS), jnp.bfloat16),
            pltpu.VMEM((chunks, block, COLUMNS), jnp.bfloat16),
            pltpu.SemaphoreType.DMA((2,)),
            pltpu.SemaphoreType.DMA((n, 2, 6)),
            pltpu.SemaphoreType.DMA((n, 2)),
            pltpu.SemaphoreType.DMA((chunks,)),
            pltpu.SemaphoreType.DMA((chunks,)),
            pltpu.SemaphoreType.DMA((chunks,)),
        ],
        compiler_params=pltpu.CompilerParams(
            collective_id=0, has_side_effects=True, vmem_limit_bytes=56 * 1024 * 1024
        ),
        cost_estimate=pl.CostEstimate(
            flops=4 * pairs * block * block * width + 2 * rows * width * model,
            bytes_accessed=2 * (w_out.size + block * model),
            transcendentals=pairs * block * width,
        ),
        name="attend_and_project",
    )(doc_lengths, queries, keys, values, w_out)


def solution(mesh):
    in_specs = (
        P("kvh", "ctx", None),
        P("kvh", "ctx", None),
        P("kvh", "ctx", None),
        P(),
        P("kvh", None),
    )
    out_specs = P(("ctx", "kvh"), None)
    return jax.shard_map(
        functools.partial(on_device, mesh.shape["ctx"]),
        mesh=mesh,
        in_specs=in_specs,
        out_specs=out_specs,
        check_vma=False,
    )
```

```python
import functools
import math

import jax
import jax.numpy as jnp
from jax import lax
from jax.experimental import pallas as pl
from jax.experimental.pallas import tpu as pltpu
from jax.sharding import PartitionSpec as P

MESH = pl.DeviceIdType.MESH
NEG = -1e30
FLOOR = -1e20
COLUMNS = 2048
LAG = 2


def grid_of(n):
    z = 4 if n % 4 == 0 else 1
    rest = n // z
    x = max(i for i in range(1, math.isqrt(rest) + 1) if rest % i == 0)
    return z, rest // x, x


def div(a, k):
    return a >> (k.bit_length() - 1) if k & (k - 1) == 0 else a // k


def mod(a, k):
    return a & (k - 1) if k & (k - 1) == 0 else a % k


def nearest(p, k, size):
    m = jnp.minimum(p, size - 1 - p)
    half = div(k + 1, 2)
    near = jnp.where(mod(k, 2) == 1, p + half, p - half)
    far = jnp.where(p < size - 1 - p, k, size - 1 - k)
    return jnp.where(k <= 2 * m, near, far)


def kernel(
    n,
    docs,
    lengths,
    q_hbm,
    k_ref,
    v_ref,
    w_hbm,
    out_hbm,
    kv,
    q_in,
    q_t,
    top,
    den,
    acc,
    att,
    w,
    mine,
    outgoing,
    incoming,
    result,
    local_sem,
    send_sem,
    recv_sem,
    part_send,
    part_recv,
    out_sem,
):
    sizes = grid_of(n)
    Z, Y, X = sizes
    block = k_ref.shape[1] // 2
    hd = k_ref.shape[2]
    width = q_in.shape[1]
    heads = width // hd
    me = lax.axis_index("ctx")
    core = lax.axis_index("kvh")
    place = (div(me, Y * X), mod(div(me, X), Y), mod(me, X))
    strides = (Y * X, X, 1)

    q_copy = pltpu.make_async_copy(q_hbm.at[0], q_in, local_sem.at[0])
    q_copy.start()
    w_copy = pltpu.make_async_copy(w_hbm, w, local_sem.at[1])

    barrier = pltpu.get_barrier_semaphore()
    count = jnp.int32(1)
    pl.semaphore_signal(
        barrier, inc=1, device_id={"kvh": 1 - core}, device_id_type=MESH
    )
    for axis in range(3):
        for step in (1, -1):
            there = place[axis] + step
            exists = (there >= 0) & (there < sizes[axis])
            count = count + exists.astype(jnp.int32)

            @pl.when(exists)
            def _(axis=axis, step=step):
                pl.semaphore_signal(
                    barrier,
                    inc=1,
                    device_id={"ctx": me + step * strides[axis]},
                    device_id_type=MESH,
                )

    for b in range(2):
        kv[me, b, 0:block] = k_ref[0, b * block : (b + 1) * block]
        kv[me, b, block:] = v_ref[0, b * block : (b + 1) * block].T
    pl.semaphore_wait(barrier, count)

    def wanted(b, source, low, high):
        if b == 0:
            return high >= jnp.minimum(source, n - 1 - source)
        return low <= source

    def index(coords):
        return sum(c * s for c, s in zip(coords, strides))

    def tree(source, b):
        order = (0, 2, 1) if b == 0 else (0, 1, 2)
        src = (div(source, Y * X), mod(div(source, X), Y), mod(source, X))
        edges = []
        arrives = jnp.bool_(False)
        on_line = jnp.bool_(True)
        for depth in (2, 1, 0):
            axis = order[depth]
            inner = order[depth + 1 :]
            p, s = place[axis], src[axis]
            first, last = list(place), list(place)
            for a in inner:
                first[a], last[a] = 0, sizes[a] - 1
            for step in (1, -1):
                there = p + step
                first_a, last_a = (there, sizes[axis] - 1) if step == 1 else (0, there)
                first[axis], last[axis] = first_a, last_a
                exists = (there >= 0) & (there < sizes[axis])
                onward = (p >= s) if step == 1 else (p <= s)
                go = on_line & exists & onward
                go = go & wanted(b, source, index(first), index(last))
                edges.append((go, axis * 2 + (step == 1), me + step * strides[axis]))
                first[axis], last[axis] = (p, sizes[axis] - 1) if step == 1 else (0, p)
                passed = (p > s) if step == 1 else (p < s)
                arrives = arrives | (
                    on_line & passed & wanted(b, source, index(first), index(last))
                )
            on_line = on_line & (p == s)
        return edges, arrives

    def copy_of(source, b, way, target):
        return pltpu.make_async_remote_copy(
            src_ref=kv.at[source, b],
            dst_ref=kv.at[source, b],
            send_sem=send_sem.at[source, b, way],
            recv_sem=recv_sem.at[source, b],
            device_id={"ctx": target},
            device_id_type=MESH,
        )

    def pass_on(source):
        for b in range(2):
            edges, arrives = tree(source, b)

            @pl.when(arrives)
            def _(b=b):
                copy_of(source, b, 0, me).wait_recv()

            for go, way, target in reversed(edges):

                @pl.when(go)
                def _(b=b, way=way, target=target):
                    copy_of(source, b, way, target).start()

    pass_on(me)
    w_copy.start()

    q_copy.wait()
    for b in range(2):
        for h in range(heads):
            q_t[b, :, h * hd : (h + 1) * hd] = q_in[
                b * block : (b + 1) * block, h * hd : (h + 1) * hd
            ].T
    top[...] = jnp.full(top.shape, FLOOR, jnp.float32)
    den[...] = jnp.zeros(den.shape, jnp.float32)
    acc[...] = jnp.zeros(acc.shape, jnp.float32)

    own_blocks = (me, 2 * n - 1 - me)
    lanes = lax.broadcasted_iota(jnp.int32, (1, block), 1)
    query_pos = [c * block + lanes for c in own_blocks]
    doc_start = [jnp.zeros((1, block), jnp.int32) for _ in own_blocks]
    end = jnp.int32(0)
    for i in range(docs):
        length = lengths[i]
        end = end + length
        doc_start = [
            s + jnp.where(end <= p, length, 0) for s, p in zip(doc_start, query_pos)
        ]

    factor = hd ** (-0.5) * math.log2(math.e)
    rows = lax.broadcasted_iota(jnp.int32, (block, block), 0)
    group = hd

    def absorb(qb, source, blocks):
        biases, keys, vals = [], [], []
        for b in blocks:
            c = source if b == 0 else 2 * n - 1 - source
            key_pos = c * block + rows
            allowed = (key_pos <= query_pos[qb]) & (key_pos >= doc_start[qb])
            biases.append(jnp.where(allowed, 0.0, NEG))
            keys.append(kv[source, b, 0:block])
            vals.append(kv[source, b, block:])
        bias = jnp.concatenate(biases, axis=0) if len(blocks) > 1 else biases[0]
        bias = jnp.concatenate([bias] * (group // block), axis=1)
        key = jnp.concatenate(keys, axis=0) if len(blocks) > 1 else keys[0]
        val = jnp.concatenate(vals, axis=1) if len(blocks) > 1 else vals[0]
        for c in range(width // group):
            cols = slice(c * group, (c + 1) * group)
            scores = jnp.dot(key, q_t[qb, :, cols], preferred_element_type=jnp.float32)
            scores = scores + bias
            old = top[qb, :, cols]
            new = jnp.maximum(old, jnp.max(scores, axis=0, keepdims=True))
            weights = jnp.exp2((scores - new) * factor)
            rescale = jnp.exp2((old - new) * factor)
            top[qb, :, cols] = new
            den[qb, :, cols] = den[qb, :, cols] * rescale + jnp.sum(
                weights, axis=0, keepdims=True
            )
            acc[qb, :, cols] = acc[qb, :, cols] * rescale + jnp.dot(
                val, weights.astype(jnp.bfloat16), preferred_element_type=jnp.float32
            )

    plane = Y * X

    def source_at(kz, j):
        return index(
            (
                nearest(place[0], kz, Z),
                nearest(place[1], div(j, X), Y),
                nearest(place[2], mod(j, X), X),
            )
        )

    def visit(r, carry):
        kz, j = div(r, plane), mod(r, plane)
        source = source_at(kz, j)

        @pl.when((j == 0) & (kz + 1 < Z))
        def _():
            pass_on(source_at(kz + 1, 0))

        @pl.when(j > 0)
        def _():
            pass_on(source)

        low = source >= n - 1 - me
        high = source >= me

        @pl.when(source <= me)
        def _():
            absorb(0, source, (0,))

        @pl.when(low & high)
        def _():
            absorb(1, source, (0, 1))

        @pl.when(low & jnp.logical_not(high))
        def _():
            absorb(1, source, (0,))

        @pl.when(high & jnp.logical_not(low))
        def _():
            absorb(1, source, (1,))

        return carry

    lax.fori_loop(0, n, visit, 0)

    for qb in range(2):
        spot = (1 - core) if qb == 0 else core
        at = pl.multiple_of(spot * block, block)
        for h in range(heads):
            cols = slice(h * hd, (h + 1) * hd)
            o = acc[qb, :, cols] / den[qb, :, cols]
            att[pl.ds(at, block), cols] = o.T.astype(jnp.bfloat16)

    w_copy.wait()
    chunks = w.shape[1] // COLUMNS

    def part(j):
        return pltpu.make_async_remote_copy(
            src_ref=outgoing.at[j],
            dst_ref=incoming.at[j],
            send_sem=part_send.at[j],
            recv_sem=part_recv.at[j],
            device_id={"kvh": 1 - core},
            device_id_type=MESH,
        )

    def store(j):
        at = pl.multiple_of(j * COLUMNS, COLUMNS)
        return pltpu.make_async_copy(
            result.at[j], out_hbm.at[:, pl.ds(at, COLUMNS)], out_sem.at[j]
        )

    def finish(j):
        part(j).wait_recv()
        total = mine[j] + incoming[j].astype(jnp.float32)
        result[j] = total.astype(jnp.bfloat16)
        store(j).start()

    def project(j, carry):
        at = pl.multiple_of(j * COLUMNS, COLUMNS)
        both = jnp.dot(
            att[...], w[:, pl.ds(at, COLUMNS)], preferred_element_type=jnp.float32
        )
        outgoing[j] = both[:block].astype(jnp.bfloat16)
        part(j).start()
        mine[j] = both[block:]

        @pl.when(j >= LAG)
        def _():
            finish(j - LAG)

        return carry

    lax.fori_loop(0, chunks, project, 0)

    def tail(j, carry):
        finish(j)
        return carry

    lax.fori_loop(chunks - LAG, chunks, tail, 0)

    def sent(source, carry):
        for b in range(2):
            for go, way, target in tree(source, b)[0]:

                @pl.when(go)
                def _(b=b, way=way, target=target):
                    copy_of(source, b, way, target).wait_send()

        return carry

    lax.fori_loop(0, n, sent, 0)

    def stored(j, carry):
        part(j).wait_send()
        store(j).wait()
        return carry

    lax.fori_loop(0, chunks, stored, 0)


def on_device(n, queries, keys, values, doc_lengths, w_out):
    rows, hd = keys.shape[1:]
    width = queries.shape[2]
    block = rows // 2
    model = w_out.shape[1]
    chunks = model // COLUMNS
    vmem = pl.BlockSpec(memory_space=pltpu.VMEM)
    far = pl.BlockSpec(memory_space=pl.ANY)
    pairs = 2 * n + 2
    return pl.pallas_call(
        functools.partial(kernel, n, doc_lengths.shape[0]),
        out_shape=jax.ShapeDtypeStruct((block, model), jnp.bfloat16),
        in_specs=[pl.BlockSpec(memory_space=pltpu.SMEM), far, vmem, vmem, far],
        out_specs=far,
        scratch_shapes=[
            pltpu.VMEM((n, 2, 2 * block, hd), jnp.bfloat16),
            pltpu.VMEM((rows, width), jnp.bfloat16),
            pltpu.VMEM((2, hd, width), jnp.bfloat16),
            pltpu.VMEM((2, 1, width), jnp.float32),
            pltpu.VMEM((2, 1, width), jnp.float32),
            pltpu.VMEM((2, hd, width), jnp.float32),
            pltpu.VMEM((rows, width), jnp.bfloat16),
            pltpu.VMEM(w_out.shape, jnp.bfloat16),
            pltpu.VMEM((chunks, block, COLUMNS), jnp.float32),
            pltpu.VMEM((chunks, block, COLUMNS), jnp.bfloat16),
            pltpu.VMEM((chunks, block, COLUMNS), jnp.bfloat16),
            pltpu.VMEM((chunks, block, COLUMNS), jnp.bfloat16),
            pltpu.SemaphoreType.DMA((2,)),
            pltpu.SemaphoreType.DMA((n, 2, 6)),
            pltpu.SemaphoreType.DMA((n, 2)),
            pltpu.SemaphoreType.DMA((chunks,)),
            pltpu.SemaphoreType.DMA((chunks,)),
            pltpu.SemaphoreType.DMA((chunks,)),
        ],
        compiler_params=pltpu.CompilerParams(
            collective_id=0, has_side_effects=True, vmem_limit_bytes=56 * 1024 * 1024
        ),
        cost_estimate=pl.CostEstimate(
            flops=4 * pairs * block * block * width + 2 * rows * width * model,
            bytes_accessed=2 * (w_out.size + block * model),
            transcendentals=pairs * block * width,
        ),
        name="attend_and_project",
    )(doc_lengths, queries, keys, values, w_out)


def solution(mesh):
    in_specs = (
        P("kvh", "ctx", None),
        P("kvh", "ctx", None),
        P("kvh", "ctx", None),
        P(),
        P("kvh", None),
    )
    out_specs = P(("ctx", "kvh"), None)
    return jax.shard_map(
        functools.partial(on_device, mesh.shape["ctx"]),
        mesh=mesh,
        in_specs=in_specs,
        out_specs=out_specs,
        check_vma=False,
    )
```
